32 devices in a mesh: grp: 8 (over y, x, core), dev: 4 (over z).
Axes of the slice: x: 2, y: 2, z: 4, core: 2. Of those that a mesh axis runs over, the one named last changes fastest.
Arguments:
- design: float32 [16384, 1024], P(('grp', 'dev')), as said below
- observed: float32 [16384], P(('grp', 'dev')), may hold values from -6 to 6
- row_weight: float32 [16384], P(('grp', 'dev')), may hold values from 0.3 to 3
- arc_of_row: int32 [16384, 1], P(('grp', 'dev')), may hold values from 0 to 7, as said below
- prior_factor: float32 [1024, 1024], P('dev'), as said below
- prior_rhs: float32 [1024], P('dev'), may hold values from -6 to 6
Outputs:
- new_factor: float32 [1024, 1024], P('dev')
- new_rhs: float32 [1024], P('dev')
The draws below stay inside these ranges and needn't reach their ends.
Inputs may be any that keep to these rules, and one draw needn't show every extreme that they name: `arc_of_row`: arc numbers count within a group of 4 devices along dev; arc a of a group is owned by the device of index a // 2 in that group. Among the rows of one device no arc stands more than 96 times. In every group the arcs of one owner stand exactly 96 times among the rows of every device of that group. `prior_factor`: upper triangular with diagonal between 1 and 2. `design`: entries below 1 in magnitude.
All inputs are finite; a program needn't handle non-finite values.
Results may differ from the reference program's by a relative error of at most 0.0013.
Values sent between devices are 32-bit elements; how exact they have to be, the bound alone decides.
A program may use at most 128 MiB of HBM per device.

```python
import math
import jax
import jax.numpy as jnp
from jax import lax

P_SIZE = 1024
ROWS_DEV = 512
ARCS_DEV = 2
ARCS_GRP = 8
MOST = 96
ROWS = 16384
N_GRP = 8
N_DEV = 4


def permute_slots(piece_key):
    return jax.random.permutation(piece_key, ARCS_GRP * MOST)


def permute_rows(piece_key):
    return jax.random.permutation(piece_key, ROWS_DEV)


def arc_labels(key):
    devices = N_GRP * N_DEV
    slot_count = ARCS_GRP * MOST
    first, second, third = jax.random.split(key, 3)
    owners = jnp.repeat(jax.random.randint(first, (N_GRP,), 0, N_DEV), N_DEV)
    slot_arc = jnp.arange(slot_count, dtype=jnp.int32) // MOST
    owned = (slot_arc // ARCS_DEV)[None, :] == owners[:, None]
    ranks = jax.vmap(permute_slots)(jax.random.split(second, devices)).astype(jnp.int32)
    scores = jnp.where(owned, ranks, ranks + slot_count)
    order = jnp.argsort(scores, axis=1, stable=True)[:, :ROWS_DEV]
    chosen = (order // MOST).astype(jnp.int32)
    mixing = jax.vmap(permute_rows)(jax.random.split(third, devices))
    labels = jnp.take_along_axis(chosen, mixing, axis=1)
    return labels.reshape(devices * ROWS_DEV, 1).astype(jnp.int32)


def draw_arc_of_row(key, part):
    return arc_labels(key)


def draw_design(key, part):
    labels = arc_labels(key)[:, 0]
    key = jax.random.fold_in(key, 11)
    first, second, third, fourth, fifth = jax.random.split(key, 5)
    groups = jnp.arange(ROWS, dtype=jnp.int32) // (ROWS_DEV * N_DEV)
    global_arc = groups * ARCS_GRP + labels
    arc_total = ARCS_GRP * N_GRP
    signs = (jax.random.randint(fifth, (1, P_SIZE), 0, 2) * 2 - 1).astype(jnp.float32)
    common = jax.random.normal(first, (arc_total, P_SIZE), jnp.float32)
    rough = jax.random.normal(second, (ROWS, P_SIZE), jnp.float32)
    shared_col = signs * jnp.exp(jax.random.uniform(third, (1, P_SIZE), jnp.float32, math.log(0.6), math.log(1.4)))
    row_factor = jax.random.normal(fourth, (ROWS, 1), jnp.float32)
    shared_scale = 4.5
    values = (jnp.take(common, global_arc, axis=0) + rough + shared_scale * row_factor * shared_col) * (1.0 / math.sqrt(ROWS))
    return jnp.clip(values, -0.99, 0.99)


def draw_prior_factor(key, part):
    key = jax.random.fold_in(key, 7)
    first, second = jax.random.split(key)
    row_index = jnp.arange(P_SIZE)[:, None]
    col_index = jnp.arange(P_SIZE)[None, :]
    diag = jnp.exp(jax.random.uniform(first, (P_SIZE,), jnp.float32, 0.0, math.log(2.0)))
    offdiag = jax.random.normal(second, (P_SIZE, P_SIZE), jnp.float32) * (0.3 / math.sqrt(P_SIZE))
    upper = jnp.where(col_index > row_index, offdiag, 0.0)
    return upper + jnp.where(col_index == row_index, diag[None, :], 0.0)


def level_of(key, dims, shards, low, top_value):
    def one(dim, shards_of):
        draws = jax.random.uniform(jax.random.fold_in(jax.random.fold_in(key, 6), dim), (shards_of,), jnp.float32, low / len(shards), top_value / len(shards))
        return jnp.repeat(jnp.exp(draws), dims[dim] // shards_of).reshape((-1,) + (1,) * (len(dims) - dim - 1))

    gain = one(*shards[0])
    for cut in shards[1:]:
        gain = gain * one(*cut)
    return gain


def bell_draw(rng, shape, spread, most, cuts=(), kind=jnp.bfloat16):
    result = jax.random.normal(rng, shape, jnp.float32) * spread
    if len(cuts) > 0:
        result = level_of(rng, shape, cuts, -0.22, 0.18) * result
    return jnp.clip(result, min=-most, max=most).astype(kind)


def setup_inputs(seed: int = 0) -> dict:
    key_of = jax.random.split(jax.random.key(seed), 7)
    return {
        "design": draw_design(jax.random.fold_in(key_of[6], 71), 0),
        "observed": bell_draw(key_of[1], (ROWS,), 1.0, 6.0, ((0, 32),), jnp.float32),
        "row_weight": jnp.clip(jnp.exp(math.log(3.0) - 2.3025851 * jax.random.uniform(key_of[2], (ROWS,), jnp.float32) ** level_of(key_of[2], (ROWS,), ((0, 32),), -0.2, 0.2)), 0.3, 3.0),
        "arc_of_row": draw_arc_of_row(jax.random.fold_in(key_of[6], 71), 0),
        "prior_factor": draw_prior_factor(jax.random.fold_in(key_of[6], 71), 0),
        "prior_rhs": bell_draw(key_of[5], (P_SIZE,), 1.0, 6.0, ((0, 4),), jnp.float32),
    }


bias_prior = 1.0

def inner(left, right):
    return lax.dot_general(left.astype(jnp.float32), right.astype(jnp.float32), (((0,), (0,)), ((), ())), precision=lax.Precision.HIGHEST, preferred_element_type=jnp.float32)

def reference(design, observed, row_weight, arc_of_row, prior_factor, prior_rhs):
    rows_all = design.shape[0]
    groups = jnp.arange(rows_all, dtype=jnp.int32) // (ROWS_DEV * N_DEV)
    arc_ids = (groups * ARCS_GRP + arc_of_row[:, 0]).astype(jnp.int32)
    arc_count = ARCS_GRP * N_GRP
    weighted = row_weight[:, None] * design
    scaled_obs = row_weight * observed
    arc_sum = jax.ops.segment_sum(row_weight[:, None] * weighted, arc_ids, arc_count)
    total = jax.ops.segment_sum(row_weight * row_weight, arc_ids, arc_count) + bias_prior
    obs_sum = jax.ops.segment_sum(row_weight * scaled_obs, arc_ids, arc_count)
    gram = inner(weighted, weighted) + inner(prior_factor, prior_factor) - inner(arc_sum / total[:, None], arc_sum)
    projected = inner(weighted, scaled_obs) + inner(prior_factor, prior_rhs) - inner(arc_sum, obs_sum / total)
    lower = jnp.linalg.cholesky(gram)
    solved = lax.linalg.triangular_solve(lower, projected[:, None], left_side=True, lower=True)
    return (lower.T, solved[:, 0])
```

```python
import functools

import jax
import jax.numpy as jnp
from jax import lax
from jax.experimental import pallas as pl
from jax.experimental.pallas import tpu as pltpu
from jax.sharding import PartitionSpec as P

ARCS_DEV = 2
BLOCK = 128
SLAB = 8

bias_prior = 1.0


def inner(left, right):
    return lax.dot_general(
        left,
        right,
        (((0,), (0,)), ((), ())),
        precision=lax.Precision.HIGH,
        preferred_element_type=jnp.float32,
    )


def dot(left, right, contract):
    return lax.dot_general(
        left,
        right,
        (((contract,), (0,)), ((), ())),
        precision=lax.Precision.HIGHEST,
        preferred_element_type=jnp.float32,
    )


def lane(x, c):
    return jnp.broadcast_to(x[:, c : c + 1], (SLAB, BLOCK))


def row(x, i):
    return jnp.broadcast_to(x[i : i + 1, :], (SLAB, BLOCK))


def factor_block(block, beside):
    slabs = BLOCK // SLAB
    sub = lax.broadcasted_iota(jnp.int32, (SLAB, BLOCK), 0)
    col = lax.broadcasted_iota(jnp.int32, (SLAB, BLOCK), 1)
    main = [block[SLAB * m : SLAB * (m + 1), :] for m in range(slabs)]
    side = [(col == sub + SLAB * m).astype(jnp.float32) for m in range(slabs)]
    upper, inverse = [], []
    for k in range(slabs):
        a, s = main[k], side[k]
        coef = [lane(a, SLAB * k + j) for j in range(SLAB)]
        up, inv = a, s
        for i in range(SLAB):
            here = sub == i
            pivot = coef[i]
            value = row(pivot, i)
            root = lax.rsqrt(value)
            root = root * (1.5 - 0.5 * value * root * root)
            recip = root * root
            row_a, row_s = row(a, i), row(s, i)
            up = jnp.where(here, row_a * root, up)
            inv = jnp.where(here, row_s * root, inv)
            for j in range(i + 1, SLAB):
                e = row(coef[j], i) * recip
                coef[j] = jnp.where(here, e, coef[j] - pivot * e)
            z_a, z_s = row_a * recip, row_s * recip
            a = jnp.where(here, z_a, a - pivot * z_a)
            s = jnp.where(here, z_s, s - pivot * z_s)
        upper.append(jnp.where(col >= sub + SLAB * k, up, 0.0))
        inverse.append(inv)
        rows_a = [row(a, j) for j in range(SLAB)]
        rows_s = [row(s, j) for j in range(SLAB)]
        for m in range(k + 1, slabs):
            c = [lane(main[m], SLAB * k + j) for j in range(SLAB)]
            for j in range(SLAB):
                main[m] = main[m] - c[j] * rows_a[j]
                side[m] = side[m] - c[j] * rows_s[j]
        beside(k)
    return jnp.concatenate(upper, axis=0), jnp.concatenate(inverse, axis=0)


def chunks(wide):
    out, at = [], 0
    while at < wide:
        step = min(2 * BLOCK, wide - at)
        out.append((at, step))
        at += step
    return out


def cholesky_kernel(g_ref, u_ref, ahead, panel):
    width, wide = g_ref.shape
    panels = width // BLOCK
    parts = chunks(wide)
    u_ref[...] = jnp.zeros_like(u_ref)
    ahead[...] = g_ref[0:BLOCK, :]

    def body(p, carry):
        here = pl.ds(pl.multiple_of(p * BLOCK, BLOCK), BLOCK)
        before = pl.ds(pl.multiple_of(jnp.maximum(p - 1, 0) * BLOCK, BLOCK), BLOCK)
        after = pl.ds(pl.multiple_of(jnp.minimum(p + 1, panels - 1) * BLOCK, BLOCK), BLOCK)
        left = u_ref[before, here]
        diag = ahead[:, here] - dot(left, left, 0)
        for at, step in parts:
            cut = pl.ds(at, step)
            panel[:, cut] = ahead[:, cut] - dot(left, u_ref[before, cut], 0)

        def beside(k):
            if k % 3 == 0 and k // 3 < len(parts):
                at, step = parts[k // 3]
                cut = pl.ds(at, step)
                ahead[:, cut] = g_ref[after, cut] - dot(
                    u_ref[:, after], u_ref[:, cut], 0
                )

        upper, inverse = factor_block(diag, beside)
        for at, step in parts:
            cut = pl.ds(at, step)
            new = dot(inverse, panel[:, cut], 1)
            columns = lax.broadcasted_iota(jnp.int32, (BLOCK, step), 1) + at
            new = jnp.where(columns >= p * BLOCK, new, 0.0)
            u_ref[here, cut] = new
        u_ref[here, here] = upper
        return carry

    lax.fori_loop(0, panels, body, 0)


def cholesky(gram):
    width, wide = gram.shape
    return pl.pallas_call(
        cholesky_kernel,
        out_shape=jax.ShapeDtypeStruct((width, wide), jnp.float32),
        in_specs=[pl.BlockSpec(memory_space=pltpu.VMEM)],
        out_specs=pl.BlockSpec(memory_space=pltpu.VMEM),
        scratch_shapes=[
            pltpu.VMEM((BLOCK, wide), jnp.float32),
            pltpu.VMEM((BLOCK, wide), jnp.float32),
        ],
        compiler_params=pltpu.CompilerParams(vmem_limit_bytes=40 * 2**20),
    )(gram)


def on_device(design, observed, row_weight, arc_of_row, prior_factor, prior_rhs):
    n_dev, n_grp = lax.axis_size("dev"), lax.axis_size("grp")
    dev, grp = lax.axis_index("dev"), lax.axis_index("grp")
    row_count, width = design.shape
    arcs_group = ARCS_DEV * n_dev
    column = row_weight[:, None]
    scaled_obs = column * observed[:, None]
    pad = jnp.zeros((row_count, BLOCK - 2), jnp.float32)
    weighted = jnp.concatenate([column * design, scaled_obs, column, pad], axis=1)
    onehot = arc_of_row == jnp.arange(arcs_group, dtype=jnp.int32)[None, :]
    arcs = lax.psum(inner(jnp.where(onehot, column, 0.0), weighted), "dev")
    arcs = lax.dynamic_slice_in_dim(arcs, dev * ARCS_DEV, ARCS_DEV, 0)
    total = arcs[:, width + 1 : width + 2] + bias_prior
    prior_rows = width // (n_dev * n_grp)
    prior = jnp.concatenate(
        [prior_factor, prior_rhs[:, None], jnp.zeros((prior_factor.shape[0], BLOCK - 1), jnp.float32)],
        axis=1,
    )
    prior = lax.dynamic_slice_in_dim(prior, grp * prior_rows, prior_rows, 0)
    left = jnp.concatenate([weighted[:, :width], prior[:, :width], -arcs[:, :width] / total], axis=0)
    right = jnp.concatenate([weighted, prior, arcs], axis=0)
    gram = lax.psum(inner(left, right), ("grp", "dev"))
    factor = cholesky(gram)
    share = width // n_dev
    rows = lax.dynamic_slice_in_dim(factor, dev * share, share, 0)
    return rows[:, :width], rows[:, width]


def solution(mesh):
    placed = (
        P(("grp", "dev"), None),
        P(("grp", "dev")),
        P(("grp", "dev")),
        P(("grp", "dev"), None),
        P("dev", None),
        P("dev"),
    )
    return jax.shard_map(
        on_device, mesh=mesh, in_specs=placed, out_specs=(P("dev", None), P("dev")), check_vma=False
    )
```

```python
import functools

import jax
import jax.numpy as jnp
from jax import lax
from jax.experimental import pallas as pl
from jax.experimental.pallas import tpu as pltpu
from jax.sharding import PartitionSpec as P

ARCS_DEV = 2
BLOCK = 128
SLAB = 8

bias_prior = 1.0


def inner(left, right):
    return lax.dot_general(
        left,
        right,
        (((0,), (0,)), ((), ())),
        precision=lax.Precision.HIGH,
        preferred_element_type=jnp.float32,
    )


def dot(left, right, contract):
    return lax.dot_general(
        left,
        right,
        (((contract,), (0,)), ((), ())),
        precision=lax.Precision.HIGHEST,
        preferred_element_type=jnp.float32,
    )


def lane(x, c):
    return jnp.broadcast_to(x[:, c : c + 1], (SLAB, BLOCK))


def row(x, i):
    return jnp.broadcast_to(x[i : i + 1, :], (SLAB, BLOCK))


def factor_block(block, beside):
    slabs = BLOCK // SLAB
    sub = lax.broadcasted_iota(jnp.int32, (SLAB, BLOCK), 0)
    col = lax.broadcasted_iota(jnp.int32, (SLAB, BLOCK), 1)
    main = [block[SLAB * m : SLAB * (m + 1), :] for m in range(slabs)]
    side = [(col == sub + SLAB * m).astype(jnp.float32) for m in range(slabs)]
    upper, inverse = [], []
    for k in range(slabs):
        a, s = main[k], side[k]
        coef = [lane(a, SLAB * k + j) for j in range(SLAB)]
        up, inv = a, s
        for i in range(SLAB):
            here = sub == i
            pivot = coef[i]
            value = row(pivot, i)
            root = lax.rsqrt(value)
            root = root * (1.5 - 0.5 * value * root * root)
            recip = root * root
            row_a, row_s = row(a, i), row(s, i)
            up = jnp.where(here, row_a * root, up)
            inv = jnp.where(here, row_s * root, inv)
            for j in range(i + 1, SLAB):
                e = row(coef[j], i) * recip
                coef[j] = jnp.where(here, e, coef[j] - pivot * e)
            z_a, z_s = row_a * recip, row_s * recip
            a = jnp.where(here, z_a, a - pivot * z_a)
            s = jnp.where(here, z_s, s - pivot * z_s)
        upper.append(jnp.where(col >= sub + SLAB * k, up, 0.0))
        inverse.append(inv)
        rows_a = [row(a, j) for j in range(SLAB)]
        rows_s = [row(s, j) for j in range(SLAB)]
        for m in range(k + 1, slabs):
            c = [lane(main[m], SLAB * k + j) for j in range(SLAB)]
            for j in range(SLAB):
                main[m] = main[m] - c[j] * rows_a[j]
                side[m] = side[m] - c[j] * rows_s[j]
        beside(k)
    return jnp.concatenate(upper, axis=0), jnp.concatenate(inverse, axis=0)


def chunks(wide):
    out, at = [], 0
    while at < wide:
        step = min(2 * BLOCK, wide - at)
        out.append((at, step))
        at += step
    return out


def cholesky_kernel(g_ref, u_ref, ahead, panel):
    width, wide = g_ref.shape
    panels = width // BLOCK
    parts = chunks(wide)
    u_ref[...] = jnp.zeros_like(u_ref)
    ahead[...] = g_ref[0:BLOCK, :]

    def body(p, carry):
        here = pl.ds(pl.multiple_of(p * BLOCK, BLOCK), BLOCK)
        before = pl.ds(pl.multiple_of(jnp.maximum(p - 1, 0) * BLOCK, BLOCK), BLOCK)
        after = pl.ds(pl.multiple_of(jnp.minimum(p + 1, panels - 1) * BLOCK, BLOCK), BLOCK)
        left = u_ref[before, here]
        diag = ahead[:, here] - dot(left, left, 0)
        for at, step in parts:
            cut = pl.ds(at, step)
            panel[:, cut] = ahead[:, cut] - dot(left, u_ref[before, cut], 0)

        def beside(k):
            if k % 3 == 0 and k // 3 < len(parts):
                at, step = parts[k // 3]
                cut = pl.ds(at, step)
                ahead[:, cut] = g_ref[after, cut] - dot(
                    u_ref[:, after], u_ref[:, cut], 0
                )

        upper, inverse = factor_block(diag, beside)
        for at, step in parts:
            cut = pl.ds(at, step)
            new = dot(inverse, panel[:, cut], 1)
            columns = lax.broadcasted_iota(jnp.int32, (BLOCK, step), 1) + at
            new = jnp.where(columns >= p * BLOCK, new, 0.0)
            u_ref[here, cut] = new
        u_ref[here, here] = upper
        return carry

    lax.fori_loop(0, panels, body, 0)


def cholesky(gram):
    width, wide = gram.shape
    return pl.pallas_call(
        cholesky_kernel,
        out_shape=jax.ShapeDtypeStruct((width, wide), jnp.float32),
        in_specs=[pl.BlockSpec(memory_space=pltpu.VMEM)],
        out_specs=pl.BlockSpec(memory_space=pltpu.VMEM),
        scratch_shapes=[
            pltpu.VMEM((BLOCK, wide), jnp.float32),
            pltpu.VMEM((BLOCK, wide), jnp.float32),
        ],
        compiler_params=pltpu.CompilerParams(vmem_limit_bytes=40 * 2**20),
    )(gram)


def packed(gram):
    width, wide = gram.shape
    panels = width // BLOCK

    def cut(p):
        return gram[p * BLOCK : (p + 1) * BLOCK, p * BLOCK :]

    return jnp.concatenate(
        [
            jnp.concatenate([cut(p), cut(panels - 1 - p)], axis=1)
            for p in range(panels // 2)
        ],
        axis=0,
    )


def unpacked(pack, width, wide):
    panels = width // BLOCK
    rows = []
    for p in range(panels):
        q = min(p, panels - 1 - p)
        size = wide - p * BLOCK
        at = 0 if p == q else pack.shape[1] - size
        piece = pack[q * BLOCK : (q + 1) * BLOCK, at : at + size]
        rows.append(jnp.pad(piece, ((0, 0), (p * BLOCK, 0))))
    return jnp.concatenate(rows, axis=0)


def sum_kernel(orders, cuts, g_ref, out_ref, acc, recv, send_sem, recv_sem, back_send, back_recv):
    rows = g_ref.shape[0]
    me = {"grp": lax.axis_index("grp"), "dev": lax.axis_index("dev")}

    def bit_of(axis, bit):
        return lax.rem(me[axis] // bit, 2)

    def partner(axis, bit):
        return {axis: me[axis] + bit * (1 - 2 * bit_of(axis, bit))}

    barrier = pltpu.get_barrier_semaphore()
    for axis, bit in orders[0]:
        pl.semaphore_signal(
            barrier, inc=1, device_id=partner(axis, bit), device_id_type=pl.DeviceIdType.MESH
        )
    pl.semaphore_wait(barrier, len(orders[0]))

    def add(source, keep, slot, size, lanes):
        step = min(size, 16)

        def body(i, carry):
            at = pl.ds(pl.multiple_of(keep + i * step, 8), step)
            got = pl.ds(pl.multiple_of(slot + i * step, 8), step)
            acc[at, lanes] = source[at, lanes] + recv[got, lanes]
            return carry

        lax.fori_loop(0, size // step, body, 0)

    base = [0 for _ in orders]
    size, slot = rows, 0
    trail = []
    for s in range(len(orders[0])):
        source = g_ref if s == 0 else acc
        halve = size >= 16
        part = size // 2 if halve else size
        copies, keeps = [], []
        for h, (order, (start, count)) in enumerate(zip(orders, cuts)):
            axis, bit = order[s]
            lanes = pl.ds(start, count)
            mine = bit_of(axis, bit)
            keep = base[h] + mine * part if halve else base[h]
            away = base[h] + (1 - mine) * part if halve else base[h]
            copy = pltpu.make_async_remote_copy(
                src_ref=source.at[pl.ds(pl.multiple_of(away, 8), part), lanes],
                dst_ref=recv.at[pl.ds(slot, part), lanes],
                send_sem=send_sem.at[s, h],
                recv_sem=recv_sem.at[s, h],
                device_id=partner(axis, bit),
                device_id_type=pl.DeviceIdType.MESH,
            )
            copy.start()
            copies.append(copy)
            keeps.append(keep)
        for h, (start, count) in enumerate(cuts):
            copies[h].wait()
            add(source, keeps[h], slot, part, pl.ds(start, count))
        if halve:
            trail.append((s, part))
        base, size, slot = keeps, part, slot + part

    for h, (start, count) in enumerate(cuts):
        at = pl.ds(pl.multiple_of(base[h], 8), size)
        out_ref[at, pl.ds(start, count)] = acc[at, pl.ds(start, count)]
    for s, part in reversed(trail):
        copies = []
        for h, (order, (start, count)) in enumerate(zip(orders, cuts)):
            axis, bit = order[s]
            region = out_ref.at[pl.ds(pl.multiple_of(base[h], 8), part), pl.ds(start, count)]
            copy = pltpu.make_async_remote_copy(
                src_ref=region,
                dst_ref=region,
                send_sem=back_send.at[s, h],
                recv_sem=back_recv.at[s, h],
                device_id=partner(axis, bit),
                device_id_type=pl.DeviceIdType.MESH,
            )
            copy.start()
            copies.append(copy)
            base[h] = base[h] - bit_of(axis, bit) * part
        for copy in copies:
            copy.wait()


def sum_all(pack, n_grp, n_dev):
    rows, lanes = pack.shape
    grp = [("grp", 1 << i) for i in range(n_grp.bit_length() - 1)]
    dev = [("dev", 1 << i) for i in range(n_dev.bit_length() - 1)]
    orders = (grp + dev, grp[:1] + grp[:0:-1] + dev)
    first = lanes // (2 * BLOCK) * BLOCK
    cuts = ((0, first), (first, lanes - first))
    slots, size = 0, rows
    for _ in orders[0]:
        size = size // 2 if size >= 16 else size
        slots += size
    sems = pltpu.SemaphoreType.DMA((len(orders[0]), 2))
    return pl.pallas_call(
        functools.partial(sum_kernel, orders, cuts),
        out_shape=jax.ShapeDtypeStruct(pack.shape, jnp.float32),
        in_specs=[pl.BlockSpec(memory_space=pltpu.VMEM)],
        out_specs=pl.BlockSpec(memory_space=pltpu.VMEM),
        scratch_shapes=[
            pltpu.VMEM((rows, lanes), jnp.float32),
            pltpu.VMEM((slots, lanes), jnp.float32),
            sems,
            sems,
            sems,
            sems,
        ],
        compiler_params=pltpu.CompilerParams(
            collective_id=0, has_side_effects=True, vmem_limit_bytes=40 * 2**20
        ),
    )(pack)


def on_device(design, observed, row_weight, arc_of_row, prior_factor, prior_rhs):
    n_dev, n_grp = lax.axis_size("dev"), lax.axis_size("grp")
    dev, grp = lax.axis_index("dev"), lax.axis_index("grp")
    row_count, width = design.shape
    arcs_group = ARCS_DEV * n_dev
    column = row_weight[:, None]
    scaled_obs = column * observed[:, None]
    pad = jnp.zeros((row_count, BLOCK - 2), jnp.float32)
    weighted = jnp.concatenate([column * design, scaled_obs, column, pad], axis=1)
    onehot = arc_of_row == jnp.arange(arcs_group, dtype=jnp.int32)[None, :]
    arcs = lax.psum(inner(jnp.where(onehot, column, 0.0), weighted), "dev")
    arcs = lax.dynamic_slice_in_dim(arcs, dev * ARCS_DEV, ARCS_DEV, 0)
    total = arcs[:, width + 1 : width + 2] + bias_prior
    prior_rows = width // (n_dev * n_grp)
    prior = jnp.concatenate(
        [prior_factor, prior_rhs[:, None], jnp.zeros((prior_factor.shape[0], BLOCK - 1), jnp.float32)],
        axis=1,
    )
    prior = lax.dynamic_slice_in_dim(prior, grp * prior_rows, prior_rows, 0)
    left = jnp.concatenate([weighted[:, :width], prior[:, :width], -arcs[:, :width] / total], axis=0)
    right = jnp.concatenate([weighted, prior, arcs], axis=0)
    pack = sum_all(packed(inner(left, right)), n_grp, n_dev)
    gram = unpacked(pack, width, width + BLOCK)
    factor = cholesky(gram)
    share = width // n_dev
    rows = lax.dynamic_slice_in_dim(factor, dev * share, share, 0)
    return rows[:, :width], rows[:, width]


def solution(mesh):
    placed = (
        P(("grp", "dev"), None),
        P(("grp", "dev")),
        P(("grp", "dev")),
        P(("grp", "dev"), None),
        P("dev", None),
        P("dev"),
    )
    return jax.shard_map(
        on_device, mesh=mesh, in_specs=placed, out_specs=(P("dev", None), P("dev")), check_vma=False
    )
```
